128 devices in a mesh: dp: 8 (over z, core), shard: 16 (over x, y).
Axes of the slice: x: 4, y: 4, z: 4, core: 2. Of those that a mesh axis runs over, the one named last changes fastest.
Arguments:
- attention_grad: float32 [8, 3968, 3968], P('dp', 'shard'), may hold values from -127 to 127
- attention_error: float32 [8, 3968, 3968], P('dp', 'shard'), may hold values from -64 to 64
- attention_warm: float32 [32, 3968], replicated, may hold values from -6 to 6
- feedforward_grad: float32 [8, 7936, 2048], P('dp', 'shard'), may hold values from -127 to 127
- feedforward_error: float32 [8, 7936, 2048], P('dp', 'shard'), may hold values from -64 to 64
- feedforward_warm: float32 [32, 2048], replicated, may hold values from -6 to 6
Outputs:
- attention_carry: float32 [8, 3968, 3968], P('dp', 'shard')
- feedforward_carry: float32 [8, 7936, 2048], P('dp', 'shard')
- attention_basis: float32 [32, 3968], replicated
- feedforward_basis: float32 [32, 2048], replicated
The draws below stay inside these ranges and needn't reach their ends.
All inputs are finite; a program needn't handle non-finite values.
Results may differ from the reference program's by a relative error of at most 0.00025.
Values sent between devices are 32-bit elements; how exact they have to be, the bound alone decides.
A program may use at most 128 MiB of HBM per device.

```python
import jax
import jax.numpy as jnp
from jax import lax

D = 3968
FW = 7936
DW = 2048
R = 32
ITERS = 2
N_DP = 8


def scaled_field(key, replicas, rows, cols, amplitude):
    keys = jax.random.split(key, 3)
    position = jnp.arange(rows, dtype=jnp.float32) / rows
    row_scale = jnp.power(10.0, 0.5 * position + 0.5 * jax.random.uniform(keys[0], (rows,), jnp.float32))
    col_scale = jnp.power(10.0, jax.random.uniform(keys[1], (cols,), jnp.float32))
    replica_scale = jnp.power(10.0, 0.5 * jnp.arange(replicas, dtype=jnp.float32) / max(replicas - 1, 1))
    noise = jax.random.truncated_normal(keys[2], -4.0, 4.0, (replicas, rows, cols), jnp.float32)
    scale = replica_scale[:, None, None] * row_scale[None, :, None] * col_scale[None, None, :]
    return amplitude * noise * scale / 10.0


def draw_attention_grad(key, part):
    return scaled_field(jax.random.fold_in(key, 11), N_DP, D, D, 1.0)


def draw_attention_error(key, part):
    return scaled_field(jax.random.fold_in(key, 23), N_DP, D, D, 0.5)


def draw_feedforward_grad(key, part):
    return scaled_field(jax.random.fold_in(key, 37), N_DP, FW, DW, 1.0)


def draw_feedforward_error(key, part):
    return scaled_field(jax.random.fold_in(key, 41), N_DP, FW, DW, 0.5)


def scatter_about(stream_key, dims, scale, bound, kind=jnp.bfloat16):
    drawn = scale * jax.random.normal(stream_key, dims, jnp.float32)
    return jnp.clip(drawn, min=-bound, max=bound).astype(kind)


def setup_inputs(seed: int = 0) -> dict:
    seeds = jax.random.split(jax.random.key(seed), 7)
    return {
        "attention_grad": draw_attention_grad(jax.random.fold_in(seeds[6], 71), 0),
        "attention_error": draw_attention_error(jax.random.fold_in(seeds[6], 71), 0),
        "attention_warm": scatter_about(seeds[2], (R, D), 1.0, 6.0, jnp.float32),
        "feedforward_grad": draw_feedforward_grad(jax.random.fold_in(seeds[6], 71), 0),
        "feedforward_error": draw_feedforward_error(jax.random.fold_in(seeds[6], 71), 0),
        "feedforward_warm": scatter_about(seeds[5], (R, DW), 1.0, 6.0, jnp.float32),
    }


highest = lax.Precision.HIGHEST

def left_product(matrix, factor):
    return lax.dot_general(matrix.astype(jnp.float32), factor.astype(jnp.float32), (((1,), (1,)), ((), ())), precision=highest, preferred_element_type=jnp.float32)

def right_product(basis, matrix):
    return lax.dot_general(basis.astype(jnp.float32), matrix.astype(jnp.float32), (((0,), (0,)), ((), ())), precision=highest, preferred_element_type=jnp.float32)

def orthonormal(left, gram):
    lower = jnp.linalg.cholesky(gram)
    return jax.scipy.linalg.solve_triangular(lower, left.T, lower=True).T

def compress(gradient, feedback, factor):
    replicas = gradient.shape[0]
    rows = gradient.shape[1]
    basis = jnp.zeros((rows, factor.shape[0]), jnp.float32)
    for sweep in range(ITERS):
        current = factor

        def add_left(running, pieces):
            return (running + left_product(pieces[0] + pieces[1], current), None)
        left = lax.scan(add_left, jnp.zeros((rows, factor.shape[0]), jnp.float32), (gradient, feedback))[0]
        gram = right_product(left, left)
        basis = orthonormal(left, gram)

        def add_right(running, pieces):
            return (running + right_product(basis, pieces[0] + pieces[1]), None)
        summed = lax.scan(add_right, jnp.zeros(factor.shape, jnp.float32), (gradient, feedback))[0]
        factor = summed / replicas
    approx = jnp.dot(basis.astype(jnp.float32), factor.astype(jnp.float32), precision=highest, preferred_element_type=jnp.float32)
    carry = gradient + feedback - approx[None]
    return (carry, factor)

def reference(attention_grad, attention_error, attention_warm, feedforward_grad, feedforward_error, feedforward_warm):
    attention_carry, attention_basis = compress(attention_grad, attention_error, attention_warm)
    feedforward_carry, feedforward_basis = compress(feedforward_grad, feedforward_error, feedforward_warm)
    return (attention_carry, feedforward_carry, attention_basis, feedforward_basis)
```

```python
import functools

import jax
import jax.numpy as jnp
from jax import lax
from jax.experimental import pallas as pl
from jax.experimental.pallas import tpu as pltpu
from jax.sharding import PartitionSpec as P

f32, bf16 = jnp.float32, jnp.bfloat16
MESH = pl.DeviceIdType.MESH
NT = (((1,), (1,)), ((), ()))
NN = (((1,), (0,)), ((), ()))
TN = (((0,), (0,)), ((), ()))
HIGHEST = lax.Precision.HIGHEST

R = 32
HALF = 16
REPLICAS = 8
CHIPS = 64
PLANE = 16
LANES = 128
A_ROWS, A_PAD, A_COLS = 248, 256, 3968
F_ROWS, F_PAD, F_COLS = 496, 512, 2048
ROWS = A_PAD + F_PAD
A_UNITS, F_UNITS = A_COLS // LANES, F_COLS // LANES
UNITS = A_UNITS + F_UNITS
A_STEP, F_STEP = 512, 256
A_FULL, A_TAIL = A_COLS // A_STEP, A_COLS % A_STEP
F_FULL = F_COLS // F_STEP
GROUPS = ((0, 16), (16, 15), (31, 8), (39, 8))


def dot(a, b, dims):
    return lax.dot_general(a, b, dims, preferred_element_type=f32)


def exact(a, b, dims):
    return lax.dot_general(a, b, dims, precision=HIGHEST, preferred_element_type=f32)


def split(x):
    hi = x.astype(bf16)
    return hi, (x - hi.astype(f32)).astype(bf16)


def stacked(x):
    return jnp.concatenate(split(x), axis=0)


def folded(x):
    return x[:R] + x[R:]


def inverse_factors(a):
    lane = lax.broadcasted_iota(jnp.int32, (R, LANES), 1)
    row_of = lax.broadcasted_iota(jnp.int32, (R, LANES), 0)
    for k in range(R):
        row = jnp.broadcast_to(a[k : k + 1, :], (R, LANES))
        first = jnp.broadcast_to(a[:, k : k + 1], (R, LANES))
        second = jnp.broadcast_to(a[:, 64 + k : 65 + k], (R, LANES))
        column = jnp.where(lane < 64, first, second)
        pivot = jnp.broadcast_to(column[k : k + 1, :], (R, LANES))
        factor = jnp.where(row_of > k, column * (1.0 / pivot), 0.0)
        a = a - factor * row
        a = jnp.where(row_of == k, row * lax.rsqrt(pivot), a)
    return a[:, R : 2 * R], a[:, 3 * R :]


def sweeps(
    ag, ae, fg, fe, aw, fw,
    ma, mf, bt, qa, qf,
    sga, sea, sgf, sef, swa, swf, load_sem,
    acc, pbuf, pmate, pz, pfull,
    gs, zl, zp, zs, rr, zg,
    p_send, p_recv, g_send, g_recv, m_send, m_recv,
    rs_send, rs_recv, ag_send, ag_recv, fw_send, fw_recv,
):
    dp, s = lax.axis_index("dp"), lax.axis_index("shard")
    z, c = dp // 2, dp % 2
    j = s * 4 + z
    mate = (z * 2 + (1 - c), s)

    def chip(o):
        return ((o % 4) * 2 + c, o // 4)

    def a_load(col, w, k):
        at = pl.ds(col, w)
        return (
            pltpu.make_async_copy(ag.at[0, :, at], sga.at[:, at], load_sem.at[0, k]),
            pltpu.make_async_copy(ae.at[0, :, at], sea.at[:, at], load_sem.at[1, k]),
        )

    def f_load(col, w, k):
        at = pl.ds(col, w)
        return (
            pltpu.make_async_copy(fg.at[0, :, at], sgf.at[:, at], load_sem.at[0, k]),
            pltpu.make_async_copy(fe.at[0, :, at], sef.at[:, at], load_sem.at[1, k]),
        )

    load_aw = pltpu.make_async_copy(aw, swa, load_sem.at[0, 16])
    load_fw = pltpu.make_async_copy(fw, swf, load_sem.at[1, 16])
    load_aw.start()
    for k in range(A_FULL + 1):
        for copy in a_load(k * A_STEP, A_STEP if k < A_FULL else A_TAIL, k):
            copy.start()
    load_fw.start()
    for k in range(F_FULL):
        for copy in f_load(k * F_STEP, F_STEP, A_FULL + 1 + k):
            copy.start()

    barrier = pltpu.get_barrier_semaphore()

    def greet(k, _):
        pl.semaphore_signal(barrier, 1, device_id=chip((j + k) % CHIPS), device_id_type=MESH)
        return 0

    lax.fori_loop(1, CHIPS, greet, 0)
    pl.semaphore_signal(barrier, 1, device_id=mate, device_id_type=MESH)

    acc[...] = jnp.zeros_like(acc)

    def absorb(copies, sg, se, sw, m, col, w, rows, pad, base):
        for copy in copies:
            copy.wait()
        at = pl.ds(col, w)
        value = jnp.concatenate([sg[:, at] + se[:, at], jnp.zeros((pad - rows, w), f32)], axis=0)
        hi, lo = split(value)
        m[0, :, at] = hi
        m[1, :, at] = lo
        x = stacked(sw[:, at])
        acc[:, base : base + pad] += dot(x, hi, NT) + dot(x, lo, NT)

    def a_absorb(k, _):
        col = pl.multiple_of(k * A_STEP, A_STEP)
        absorb(a_load(col, A_STEP, k), sga, sea, swa, ma, col, A_STEP, A_ROWS, A_PAD, 0)
        return 0

    def f_absorb(k, _):
        col = pl.multiple_of(k * F_STEP, F_STEP)
        absorb(f_load(col, F_STEP, A_FULL + 1 + k), sgf, sef, swf, mf, col, F_STEP, F_ROWS, F_PAD, A_PAD)
        return 0

    load_aw.wait()
    lax.fori_loop(0, A_FULL, a_absorb, 0)
    absorb(a_load(A_FULL * A_STEP, A_TAIL, A_FULL), sga, sea, swa, ma, A_FULL * A_STEP, A_TAIL, A_ROWS, A_PAD, 0)
    load_fw.wait()
    lax.fori_loop(0, F_FULL, f_absorb, 0)
    pl.semaphore_wait(barrier, CHIPS)

    def units_of(it, first, count):
        def unit(u):
            return jnp.concatenate([zg[it, 0, u], zg[it, 1, u]], axis=0)

        return jnp.concatenate([unit(first + i) for i in range(count)], axis=1)

    def left_again():
        acc[...] = jnp.zeros_like(acc)

        def a_piece(first, col, w):
            x = stacked(units_of(0, first, w // LANES))
            at = pl.ds(col, w)
            acc[:, :A_PAD] += dot(x, ma[0, :, at], NT) + dot(x, ma[1, :, at], NT)

        def a_step(k, _):
            a_piece(k * (A_STEP // LANES), pl.multiple_of(k * A_STEP, A_STEP), A_STEP)
            return 0

        def f_step(k, _):
            x = stacked(units_of(0, A_UNITS + k * (F_STEP // LANES), F_STEP // LANES))
            at = pl.ds(pl.multiple_of(k * F_STEP, F_STEP), F_STEP)
            acc[:, A_PAD:] += dot(x, mf[0, :, at], NT) + dot(x, mf[1, :, at], NT)
            return 0

        lax.fori_loop(0, A_FULL, a_step, 0)
        a_piece(A_FULL * (A_STEP // LANES), A_FULL * A_STEP, A_TAIL)
        lax.fori_loop(0, F_FULL, f_step, 0)

    def remote(src, dst, send, recv, to):
        return pltpu.make_async_remote_copy(src, dst, send, recv, device_id=to, device_id_type=MESH)

    inverses = None
    left = None
    for it in range(2):
        if it == 1:
            left_again()

        pbuf[it] = folded(acc[...])
        mine, other = pl.ds(pl.multiple_of(c * HALF, HALF), HALF), pl.ds(pl.multiple_of((1 - c) * HALF, HALF), HALF)
        copy = remote(pbuf.at[it, other], pmate.at[it], p_send.at[it, 0], p_recv.at[it, 0], mate)
        copy.start()
        copy.wait()
        pz[it, z] = pbuf[it, mine] + pmate[it]
        copies = []
        for i in (2, 1, 3):
            to = (z + i) % 4
            copy = remote(pz.at[it, z], pz.at[it, z], p_send.at[it, i], p_recv.at[it, 1 + z], (to * 2 + c, s))
            copy.start()
            copies.append(copy)
        for i in (1, 3, 2):
            o = (z + i) % 4
            remote(pz.at[it, o], pz.at[it, o], p_send.at[it, i], p_recv.at[it, 1 + o], mate).wait_recv()
        pfull[it, mine] = (pz[it, 0] + pz[it, 1]) + (pz[it, 2] + pz[it, 3])
        copy = remote(pfull.at[it, mine], pfull.at[it, mine], p_send.at[it, 4], p_recv.at[it, 5], mate)
        copy.start()
        for sent in copies:
            sent.wait_send()
        copy.wait_send()
        remote(pfull.at[it, other], pfull.at[it, other], p_send.at[it, 4], p_recv.at[it, 5], mate).wait_recv()
        left = pfull[it]
        if it == 1:
            left = jnp.concatenate(
                [exact(inverses[0], left[:, :A_PAD], NN), exact(inverses[1], left[:, A_PAD:], NN)], axis=1
            ) * (1.0 / REPLICAS)

        la, lf = left[:, :A_PAD], left[:, A_PAD:]
        ga, gf = exact(la, la, NT), exact(lf, lf, NT)
        gs[it, s] = jnp.concatenate([ga[:HALF], ga[HALF:], gf[:HALF], gf[HALF:]], axis=1)

        def send_gram(k, _, it=it):
            to = (s + k) % PLANE
            remote(gs.at[it, s], gs.at[it, s], g_send.at[it, to], g_recv.at[it, s], (dp, to)).start()
            return 0

        lax.fori_loop(1, PLANE, send_gram, 0)

        pa, pf = stacked(la), stacked(lf)

        def a_right(col, first, w, it=it, pa=pa):
            at = pl.ds(col, w)
            y = folded(dot(pa, ma[0, :, at], NN)) + folded(dot(pa, ma[1, :, at], NN))
            for i in range(w // LANES):
                zl[it, 0, first + i] = y[:HALF, i * LANES : (i + 1) * LANES]
                zl[it, 1, first + i] = y[HALF:, i * LANES : (i + 1) * LANES]

        def a_right_step(k, _):
            a_right(pl.multiple_of(k * A_STEP, A_STEP), k * (A_STEP // LANES), A_STEP)
            return 0

        def f_right_step(k, _, it=it, pf=pf):
            at = pl.ds(pl.multiple_of(k * F_STEP, F_STEP), F_STEP)
            first = A_UNITS + k * (F_STEP // LANES)
            y = folded(dot(pf, mf[0, :, at], NN)) + folded(dot(pf, mf[1, :, at], NN))
            for i in range(F_STEP // LANES):
                zl[it, 0, first + i] = y[:HALF, i * LANES : (i + 1) * LANES]
                zl[it, 1, first + i] = y[HALF:, i * LANES : (i + 1) * LANES]
            return 0

        def to_mate(g, it=it):
            at = pl.ds(*GROUPS[g])
            return remote(zl.at[it, 1 - c, at], zp.at[it, at], m_send.at[it, g], m_recv.at[it, g], mate)

        lax.fori_loop(0, 4, a_right_step, 0)
        to_mate(0).start()
        lax.fori_loop(4, A_FULL, a_right_step, 0)
        a_right(A_FULL * A_STEP, A_FULL * (A_STEP // LANES), A_TAIL)
        to_mate(1).start()
        lax.fori_loop(0, 4, f_right_step, 0)
        to_mate(2).start()
        lax.fori_loop(4, F_FULL, f_right_step, 0)
        to_mate(3).start()
        for g, (first, count) in enumerate(GROUPS):
            to_mate(g).wait()
            at = pl.ds(first, count)
            zs[it, at] = zl[it, c, at] + zp[it, at]

        def scatter(k, _, it=it):
            o = (j + k) % CHIPS

            @pl.when(o < UNITS)
            def _():
                remote(zs.at[it, o], rr.at[it, j], rs_send.at[it, o], rs_recv.at[it, j], chip(o)).start()

            return 0

        lax.fori_loop(1, CHIPS, scatter, 0)

        def gram_done(k, _, it=it):
            o = (s + k) % PLANE
            remote(gs.at[it, s], gs.at[it, o], g_send.at[it, o], g_recv.at[it, o], mate).wait()
            return 0

        lax.fori_loop(1, PLANE, gram_done, 0)
        gram = gs[it, 0]
        for o in range(1, PLANE):
            gram = gram + gs[it, o]
        eye = (
            lax.broadcasted_iota(jnp.int32, (R, R), 0) == lax.broadcasted_iota(jnp.int32, (R, R), 1)
        ).astype(f32)
        ga = jnp.concatenate([gram[:, :R], gram[:, R : 2 * R]], axis=0)
        gf = jnp.concatenate([gram[:, 2 * R : 3 * R], gram[:, 3 * R :]], axis=0)
        inverses = inverse_factors(jnp.concatenate([ga, eye, gf, eye], axis=1))
        if it == 1:
            bt[...] = jnp.concatenate([exact(inverses[0], la, NN), exact(inverses[1], lf, NN)], axis=1)

        def scattered(o, _, it=it):
            @pl.when(o != j)
            def _():
                remote(zs.at[it, o], rr.at[it, o], rs_send.at[it, o], rs_recv.at[it, o], mate).wait_send()

            return 0

        lax.fori_loop(0, UNITS, scattered, 0)

        @pl.when(j < UNITS)
        def _(it=it):
            rr[it, j] = zs[it, j]

            def arrived(k, _):
                o = (j + k) % CHIPS
                remote(rr.at[it, o], rr.at[it, o], rs_send.at[it, 0], rs_recv.at[it, o], mate).wait_recv()
                return 0

            lax.fori_loop(1, CHIPS, arrived, 0)
            zg[it, c, j] = jnp.sum(rr[it], axis=0)

            def gather(k, _):
                o = (j + k) % CHIPS
                remote(zg.at[it, c, j], zg.at[it, c, j], ag_send.at[it, o], ag_recv.at[it, j], chip(o)).start()
                return 0

            lax.fori_loop(1, CHIPS, gather, 0)

            def gathered(k, _):
                o = (j + k) % CHIPS
                remote(zg.at[it, c, j], zg.at[it, c, j], ag_send.at[it, o], ag_recv.at[it, j], mate).wait_send()
                return 0

            lax.fori_loop(1, CHIPS, gathered, 0)

        for g, (first, count) in enumerate(GROUPS):

            def landed(o, _, it=it):
                @pl.when(o != j)
                def _():
                    remote(zg.at[it, c, o], zg.at[it, c, o], ag_send.at[it, 0], ag_recv.at[it, o], mate).wait_recv()

                return 0

            lax.fori_loop(first, first + count, landed, 0)
            at = pl.ds(first, count)
            remote(zg.at[it, c, at], zg.at[it, c, at], fw_send.at[it, g], fw_recv.at[it, g], mate).start()
        for g, (first, count) in enumerate(GROUPS):
            at = pl.ds(first, count)
            remote(zg.at[it, 1 - c, at], zg.at[it, 1 - c, at], fw_send.at[it, g], fw_recv.at[it, g], mate).wait()

    def normal(inverse, x):
        hi, lo = split(x)
        return dot(inverse, jnp.concatenate([hi, lo, hi, lo], axis=0), NN) * (1.0 / REPLICAS)

    def wide(inverse):
        hi, lo = split(inverse)
        return jnp.concatenate([hi, hi, lo, lo], axis=1)

    wa, wf = wide(inverses[0]), wide(inverses[1])

    def a_out(k, _):
        qa[:, pl.ds(pl.multiple_of(k * A_STEP, A_STEP), A_STEP)] = normal(wa, units_of(1, k * 4, 4))
        return 0

    def f_out(k, _):
        qf[:, pl.ds(pl.multiple_of(k * 512, 512), 512)] = normal(wf, units_of(1, A_UNITS + k * 4, 4))
        return 0

    lax.fori_loop(0, A_FULL, a_out, 0)
    qa[:, A_FULL * A_STEP :] = normal(wa, units_of(1, A_FULL * 4, 3))
    lax.fori_loop(0, 4, f_out, 0)


def carries(ma, mf, bt, qa, qf, ca, cf, oa, of, sa, sf, sem, q_sem):
    copies = [pltpu.make_async_copy(qa, oa, q_sem.at[0]), pltpu.make_async_copy(qf, of, q_sem.at[1])]
    for copy in copies:
        copy.start()
    bh, bl = split(bt[...])
    basis = jnp.concatenate([bh, bh, bl, bl], axis=0)
    n = 0
    for m, q, out, stage, rows, base, pad, cols, step in (
        (ma, qa, ca, sa, A_ROWS, 0, A_PAD, A_COLS, 512),
        (mf, qf, cf, sf, F_ROWS, A_PAD, F_PAD, F_COLS, 256),
    ):
        for col in range(0, cols, step):
            at = slice(col, min(col + step, cols))
            qh, ql = split(q[:, at])
            low = dot(basis[:, base : base + pad], jnp.concatenate([qh, ql, qh, ql], axis=0), TN)
            full = m[0, :, at].astype(f32) + m[1, :, at].astype(f32) - low
            stage[:, at] = full[:rows]
            copy = pltpu.make_async_copy(stage.at[:, at], out.at[0, :, at], sem.at[n])
            copy.start()
            copies.append(copy)
            n += 1
    for copy in copies:
        copy.wait()


def shards(ag, ae, aw, fg, fe, fw):
    hbm = pl.BlockSpec(memory_space=pl.ANY)
    vmem = pl.BlockSpec(memory_space=pltpu.VMEM)
    dma = pltpu.SemaphoreType.DMA
    ma, mf, bt, qa, qf = pl.pallas_call(
        sweeps,
        name="sweeps",
        out_shape=(
            pltpu.VMEM((2, A_PAD, A_COLS), bf16),
            pltpu.VMEM((2, F_PAD, F_COLS), bf16),
            pltpu.VMEM((R, ROWS), f32),
            pltpu.VMEM((R, A_COLS), f32),
            pltpu.VMEM((R, F_COLS), f32),
        ),
        in_specs=[hbm] * 6,
        out_specs=[vmem] * 5,
        scratch_shapes=[
            pltpu.VMEM((A_ROWS, A_COLS), f32),
            pltpu.VMEM((A_ROWS, A_COLS), f32),
            pltpu.VMEM((F_ROWS, F_COLS), f32),
            pltpu.VMEM((F_ROWS, F_COLS), f32),
            pltpu.VMEM((R, A_COLS), f32),
            pltpu.VMEM((R, F_COLS), f32),
            dma((2, 17)),
            pltpu.VMEM((2 * R, ROWS), f32),
            pltpu.VMEM((2, R, ROWS), f32),
            pltpu.VMEM((2, HALF, ROWS), f32),
            pltpu.VMEM((2, 4, HALF, ROWS), f32),
            pltpu.VMEM((2, R, ROWS), f32),
            pltpu.VMEM((2, PLANE, HALF, LANES), f32),
            pltpu.VMEM((2, 2, UNITS, HALF, LANES), f32),
            pltpu.VMEM((2, UNITS, HALF, LANES), f32),
            pltpu.VMEM((2, UNITS, HALF, LANES), f32),
            pltpu.VMEM((2, CHIPS, HALF, LANES), f32),
            pltpu.VMEM((2, 2, UNITS, HALF, LANES), f32),
            dma((2, 5)),
            dma((2, 6)),
            dma((2, PLANE)),
            dma((2, PLANE)),
            dma((2, 4)),
            dma((2, 4)),
            dma((2, CHIPS)),
            dma((2, CHIPS)),
            dma((2, CHIPS)),
            dma((2, CHIPS)),
            dma((2, 4)),
            dma((2, 4)),
        ],
        compiler_params=pltpu.CompilerParams(
            collective_id=0, has_side_effects=True, vmem_limit_bytes=46 * 2**20
        ),
    )(ag, ae, fg, fe, aw, fw)
    return tuple(
        pl.pallas_call(
            carries,
            name="carries",
            out_shape=(
                jax.ShapeDtypeStruct((1, A_ROWS, A_COLS), f32),
                jax.ShapeDtypeStruct((1, F_ROWS, F_COLS), f32),
                jax.ShapeDtypeStruct((R, A_COLS), f32),
                jax.ShapeDtypeStruct((R, F_COLS), f32),
            ),
            in_specs=[vmem] * 5,
            out_specs=[hbm] * 4,
            scratch_shapes=[
                pltpu.VMEM((A_ROWS, A_COLS), f32),
                pltpu.VMEM((F_ROWS, F_COLS), f32),
                dma((16,)),
                dma((2,)),
            ],
            compiler_params=pltpu.CompilerParams(vmem_limit_bytes=24 * 2**20),
        )(ma, mf, bt, qa, qf)
    )


def solution(mesh):
    rows = P("dp", "shard", None)
    return jax.shard_map(
        shards,
        mesh=mesh,
        in_specs=(rows, rows, P(), rows, rows, P()),
        out_specs=(rows, rows, P(), P()),
        check_vma=False,
    )
```

```python
import functools

import jax
import jax.numpy as jnp
from jax import lax
from jax.experimental import pallas as pl
from jax.experimental.pallas import tpu as pltpu
from jax.sharding import PartitionSpec as P

f32, bf16 = jnp.float32, jnp.bfloat16
MESH = pl.DeviceIdType.MESH
NT = (((1,), (1,)), ((), ()))
NN = (((1,), (0,)), ((), ()))
TN = (((0,), (0,)), ((), ()))
HIGHEST = lax.Precision.HIGHEST

R = 32
HALF = 16
REPLICAS = 8
CHIPS = 64
PLANE = 16
LANES = 128
A_ROWS, A_PAD, A_COLS = 248, 256, 3968
F_ROWS, F_PAD, F_COLS = 496, 512, 2048
ROWS = A_PAD + F_PAD
A_UNITS, F_UNITS = A_COLS // LANES, F_COLS // LANES
F_FIRST, UNITS = 32, 48
A_STEP, F_STEP = 512, 256
A_FULL, A_TAIL = A_COLS // A_STEP, A_COLS % A_STEP
F_FULL = F_COLS // F_STEP
GROUPS = ((0, 16), (16, 15), (32, 16))


def dot(a, b, dims):
    return lax.dot_general(a, b, dims, preferred_element_type=f32)


def exact(a, b, dims):
    return lax.dot_general(a, b, dims, precision=HIGHEST, preferred_element_type=f32)


def split(x):
    hi = x.astype(bf16)
    return hi, (x - hi.astype(f32)).astype(bf16)


def stacked(x):
    return jnp.concatenate(split(x), axis=0)


def folded(x):
    return x[:R] + x[R:]


def inverse_factors(a):
    lane = lax.broadcasted_iota(jnp.int32, (R, LANES), 1)
    row_of = lax.broadcasted_iota(jnp.int32, (R, LANES), 0)
    for k in range(R):
        row = jnp.broadcast_to(a[k : k + 1, :], (R, LANES))
        first = jnp.broadcast_to(a[:, k : k + 1], (R, LANES))
        second = jnp.broadcast_to(a[:, 64 + k : 65 + k], (R, LANES))
        column = jnp.where(lane < 64, first, second)
        pivot = jnp.broadcast_to(column[k : k + 1, :], (R, LANES))
        factor = jnp.where(row_of > k, column * (1.0 / pivot), 0.0)
        a = a - factor * row
        a = jnp.where(row_of == k, row * lax.rsqrt(pivot), a)
    return a[:, R : 2 * R], a[:, 3 * R :]


def sweeps(
    ag, ae, fg, fe, aw, fw,
    ma, mf, bt, qa, qf,
    sa, sf, swa, swf, load_sem, warm_sem,
    acc, a_part, f_part, a_mate, f_mate, a_z, f_z, a_sum, f_sum,
    gs, zl, zp, zs, rr, zg,
    p_send, p_recv, g_send, g_recv, m_send, m_recv,
    rs_send, rs_recv, ag_send, ag_recv, fw_send, fw_recv,
):
    dp, s = lax.axis_index("dp"), lax.axis_index("shard")
    z, c = lax.div(dp, 2), lax.rem(dp, 2)
    x, y = lax.div(s, 4), lax.rem(s, 4)
    j = s * 4 + z
    mate = (z * 2 + (1 - c), s)
    unit = lax.rem(27 * j, CHIPS)
    owner = jnp.logical_and(unit < UNITS, unit != A_UNITS)

    along = [lax.rem(z + i, 4) * 2 + c for i in range(4)]

    def each_peer(act):
        def column(k, _):
            to = lax.rem(x + 2 + lax.div(k, 4), 4) * 4 + lax.rem(y + 2 + lax.rem(k, 4), 4)
            for i in (2, 1, 3):
                act((along[i], to))

            @pl.when(to != s)
            def _():
                act((dp, to))

            return 0

        lax.fori_loop(0, PLANE, column, 0)

    def remote(src, dst, send, recv, to):
        return pltpu.make_async_remote_copy(src, dst, send, recv, device_id=to, device_id_type=MESH)

    def loads(grad, error, stage, col, w, k):
        at = pl.ds(col, w)
        return (
            pltpu.make_async_copy(grad.at[0, :, at], stage.at[0, :, at], load_sem.at[k]),
            pltpu.make_async_copy(error.at[0, :, at], stage.at[1, :, at], load_sem.at[k]),
        )

    load_aw = pltpu.make_async_copy(aw, swa, warm_sem.at[0])
    load_fw = pltpu.make_async_copy(fw, swf, warm_sem.at[1])
    load_aw.start()
    for k in range(A_FULL + 1):
        for copy in loads(ag, ae, sa, k * A_STEP, A_STEP if k < A_FULL else A_TAIL, k):
            copy.start()
    load_fw.start()
    for k in range(F_FULL):
        for copy in loads(fg, fe, sf, k * F_STEP, F_STEP, A_FULL + 1 + k):
            copy.start()

    barrier = pltpu.get_barrier_semaphore()

    def greet(to):
        pl.semaphore_signal(barrier, 1, device_id=to, device_id_type=MESH)

    each_peer(greet)
    pl.semaphore_signal(barrier, 1, device_id=mate, device_id_type=MESH)
    acc[...] = jnp.zeros_like(acc)

    def absorb(stage, sw, m, col, w, rows, pad, base, k):
        at = pl.ds(col, w)
        pltpu.make_async_copy(stage.at[:, :, at], stage.at[:, :, at], load_sem.at[k]).wait()
        value = jnp.concatenate([stage[0, :, at] + stage[1, :, at], jnp.zeros((pad - rows, w), f32)], axis=0)
        hi, lo = split(value)
        m[0, :, at] = hi
        m[1, :, at] = lo
        terms = stacked(sw[:, at])
        acc[:, base : base + pad] += dot(terms, hi, NT) + dot(terms, lo, NT)

    def a_absorb(k, _):
        absorb(sa, swa, ma, pl.multiple_of(k * A_STEP, A_STEP), A_STEP, A_ROWS, A_PAD, 0, k)
        return 0

    def f_absorb(k, _):
        col = pl.multiple_of(k * F_STEP, F_STEP)
        absorb(sf, swf, mf, col, F_STEP, F_ROWS, F_PAD, A_PAD, A_FULL + 1 + k)
        return 0

    def joined(it, first, count):
        return jnp.concatenate(
            [jnp.concatenate([zg[it, 0, first + i], zg[it, 1, first + i]], axis=0) for i in range(count)], axis=1
        )

    def a_left(first, col, w):
        terms = stacked(joined(0, first, w // LANES))
        at = pl.ds(col, w)
        acc[:, :A_PAD] += dot(terms, ma[0, :, at], NT) + dot(terms, ma[1, :, at], NT)

    def a_left_step(k, _):
        a_left(k * (A_STEP // LANES), pl.multiple_of(k * A_STEP, A_STEP), A_STEP)
        return 0

    def f_left_step(k, _):
        terms = stacked(joined(0, F_FIRST + k * (F_STEP // LANES), F_STEP // LANES))
        at = pl.ds(pl.multiple_of(k * F_STEP, F_STEP), F_STEP)
        acc[:, A_PAD:] += dot(terms, mf[0, :, at], NT) + dot(terms, mf[1, :, at], NT)
        return 0

    mine = pl.ds(pl.multiple_of(c * HALF, HALF), HALF)
    other = pl.ds(pl.multiple_of((1 - c) * HALF, HALF), HALF)
    rows_of = (slice(0, A_PAD), slice(A_PAD, ROWS))
    part, from_mate, along_z, whole = (a_part, f_part), (a_mate, f_mate), (a_z, f_z), (a_sum, f_sum)

    def halves(it, m):
        return remote(part[m].at[it, other], from_mate[m].at[it], p_send.at[it, m, 0], p_recv.at[it, m, 0], mate)

    def start_halves(it, m):
        part[m][it] = folded(acc[:, rows_of[m]])
        halves(it, m).start()

    def start_z(it, m):
        halves(it, m).wait()
        along_z[m][it, z] = part[m][it, mine] + from_mate[m][it]
        for i in (2, 1, 3):
            at = along_z[m].at[it, z]
            remote(at, at, p_send.at[it, m, 1], p_recv.at[it, m, 1], (along[i], s)).start()

    def start_back(it, m):
        three = along_z[m].at[it, pl.ds(0, 3)]
        remote(three, three, p_send.at[it, m, 1], p_recv.at[it, m, 1], mate).wait()
        terms = along_z[m]
        whole[m][it, mine] = (terms[it, 0] + terms[it, 1]) + (terms[it, 2] + terms[it, 3])
        at = whole[m].at[it, mine]
        remote(at, at, p_send.at[it, m, 2], p_recv.at[it, m, 2], mate).start()

    def finish_left(it, m, inverses):
        at = whole[m].at[it, other]
        remote(at, at, p_send.at[it, m, 2], p_recv.at[it, m, 2], mate).wait()
        left = whole[m][it]
        if it == 1:
            left = exact(inverses[m], left, NN) * (1.0 / REPLICAS)
        return left

    def keep(it, first, product):
        for i in range(product.shape[1] // LANES):
            zl[it, 0, first + i] = product[:HALF, i * LANES : (i + 1) * LANES]
            zl[it, 1, first + i] = product[HALF:, i * LANES : (i + 1) * LANES]

    def right(it, m, terms, first, col, w):
        matrix = (ma, mf)[m]
        at = pl.ds(col, w)
        keep(it, first, folded(dot(terms, matrix[0, :, at], NN)) + folded(dot(terms, matrix[1, :, at], NN)))

    def right_steps(it, m, terms, begin, end):
        def step(k, _):
            first = k * (A_STEP // LANES) + (0, F_FIRST)[m]
            right(it, m, terms, first, pl.multiple_of(k * A_STEP, A_STEP), A_STEP)
            return 0

        lax.fori_loop(begin, end, step, 0)

    def to_mate(it, g):
        at = pl.ds(*GROUPS[g])
        return remote(zl.at[it, 1 - c, at], zp.at[it, at], m_send.at[it, g], m_recv.at[it, g], mate)

    def scatter(it, g):
        first, count = GROUPS[g]
        to_mate(it, g).wait()
        at = pl.ds(first, count)
        zs[it, at] = zl[it, c, at] + zp[it, at]

        def send(k, _):
            u = first + lax.rem(j + k, count)
            o = lax.rem(19 * u, CHIPS)

            @pl.when(o != j)
            def _():
                to = (lax.rem(o, 4) * 2 + c, lax.div(o, 4))
                remote(zs.at[it, u], rr.at[it, j], rs_send.at[it], rs_recv.at[it], to).start()

            return 0

        lax.fori_loop(0, count, send, 0)

    eye = (lax.broadcasted_iota(jnp.int32, (R, R), 0) == lax.broadcasted_iota(jnp.int32, (R, R), 1)).astype(f32)

    def start_gram(it, la, lf):
        ga, gf = exact(la, la, NT), exact(lf, lf, NT)
        gs[it, s] = jnp.concatenate([ga[:HALF], ga[HALF:], gf[:HALF], gf[HALF:]], axis=1)

        def send(k, _):
            at = gs.at[it, s]
            remote(at, at, g_send.at[it], g_recv.at[it], (dp, lax.rem(s + k, PLANE))).start()
            return 0

        lax.fori_loop(1, PLANE, send, 0)

    def finish_gram(it):
        others = gs.at[it, pl.ds(0, PLANE - 1)]
        remote(others, others, g_send.at[it], g_recv.at[it], mate).wait()
        gram = gs[it, 0]
        for o in range(1, PLANE):
            gram = gram + gs[it, o]
        ga = jnp.concatenate([gram[:, :R], gram[:, R : 2 * R]], axis=0)
        gf = jnp.concatenate([gram[:, 2 * R : 3 * R], gram[:, 3 * R :]], axis=0)
        return inverse_factors(jnp.concatenate([ga, eye, gf, eye], axis=1))

    def gather(it):
        @pl.when(owner)
        def _():
            rr[it, j] = zs[it, unit]
            others = rr.at[it, pl.ds(0, CHIPS - 1)]
            remote(others, others, rs_send.at[it], rs_recv.at[it], mate).wait_recv()
            zg[it, c, unit] = jnp.sum(rr[it], axis=0)

            group = lax.div(unit, 16)

            def send(to):
                at = zg.at[it, c, unit]
                remote(at, at, ag_send.at[it], ag_recv.at[it, group], to).start()

            each_peer(send)

    def sent(it):
        @pl.when(owner)
        def _():
            some = zs.at[it, pl.ds(0, 46)]
            remote(some, some, rs_send.at[it], rs_recv.at[it], mate).wait_send()
            others = rr.at[it, pl.ds(0, CHIPS - 1)]
            remote(others, others, ag_send.at[it], rs_recv.at[it], mate).wait_send()

        @pl.when(jnp.logical_not(owner))
        def _():
            some = zs.at[it, pl.ds(0, 47)]
            remote(some, some, rs_send.at[it], rs_recv.at[it], mate).wait_send()

    def handed(it, g):
        first, count = GROUPS[g]
        at = zg.at[it, c, pl.ds(first, count)]
        return remote(at, at, fw_send.at[it, g], fw_recv.at[it, g], mate)

    def hand_on(it, g):
        first, count = GROUPS[g]
        own = jnp.logical_and(unit >= first, unit < first + count)

        @pl.when(own)
        def _():
            some = zg.at[it, c, pl.ds(first, count - 1)]
            remote(some, some, ag_send.at[it], ag_recv.at[it, g], mate).wait_recv()

        @pl.when(jnp.logical_not(own))
        def _():
            some = zg.at[it, c, pl.ds(first, count)]
            remote(some, some, ag_send.at[it], ag_recv.at[it, g], mate).wait_recv()

        handed(it, g).start()

    def normal(inverse, value):
        hi, lo = split(value)
        return dot(inverse, jnp.concatenate([hi, lo, hi, lo], axis=0), NN) * (1.0 / REPLICAS)

    def wide(inverse):
        hi, lo = split(inverse)
        return jnp.concatenate([hi, hi, lo, lo], axis=1)

    def a_out(inverse, begin, end):
        def step(k, _):
            qa[:, pl.ds(pl.multiple_of(k * A_STEP, A_STEP), A_STEP)] = normal(inverse, joined(1, k * 4, 4))
            return 0

        lax.fori_loop(begin, end, step, 0)

    def f_out(inverse):
        def step(k, _):
            qf[:, pl.ds(pl.multiple_of(k * A_STEP, A_STEP), A_STEP)] = normal(inverse, joined(1, F_FIRST + k * 4, 4))
            return 0

        lax.fori_loop(0, F_COLS // A_STEP, step, 0)

    inverses = None
    for it in range(2):
        if it == 0:
            load_aw.wait()
            lax.fori_loop(0, A_FULL, a_absorb, 0)
            absorb(sa, swa, ma, A_FULL * A_STEP, A_TAIL, A_ROWS, A_PAD, 0, A_FULL)
            pl.semaphore_wait(barrier, CHIPS)
            start_halves(it, 0)
            load_fw.wait()
            lax.fori_loop(0, 4, f_absorb, 0)
            start_z(it, 0)
            lax.fori_loop(4, F_FULL, f_absorb, 0)
        else:
            acc[...] = jnp.zeros_like(acc)
            hand_on(0, 0)
            hand_on(0, 1)
            handed(0, 0).wait()
            lax.fori_loop(0, 4, a_left_step, 0)
            hand_on(0, 2)
            handed(0, 1).wait()
            lax.fori_loop(4, A_FULL, a_left_step, 0)
            a_left(A_FULL * (A_STEP // LANES), A_FULL * A_STEP, A_TAIL)
            start_halves(it, 0)
            handed(0, 2).wait()
            lax.fori_loop(0, 4, f_left_step, 0)
            start_z(it, 0)
            lax.fori_loop(4, F_FULL, f_left_step, 0)
        start_halves(it, 1)
        if it == 0:
            start_back(it, 0)
            start_z(it, 1)
        else:
            start_z(it, 1)
            start_back(it, 0)
        la = finish_left(it, 0, inverses)
        terms = stacked(la)
        right_steps(it, 0, terms, 0, 4)
        to_mate(it, 0).start()
        right_steps(it, 0, terms, 4, A_FULL)
        right(it, 0, terms, A_FULL * (A_STEP // LANES), A_FULL * A_STEP, A_TAIL)
        to_mate(it, 1).start()
        if it == 0:
            scatter(it, 0)
            start_back(it, 1)
        else:
            start_back(it, 1)
            scatter(it, 0)
        lf = finish_left(it, 1, inverses)
        terms = stacked(lf)
        right_steps(it, 1, terms, 0, F_COLS // A_STEP)
        to_mate(it, 2).start()
        scatter(it, 1)
        scatter(it, 2)
        start_gram(it, la, lf)
        gather(it)
        inverses = finish_gram(it)
        if it == 1:
            bt[...] = jnp.concatenate([exact(inverses[0], la, NN), exact(inverses[1], lf, NN)], axis=1)
        sent(it)

    wa, wf = wide(inverses[0]), wide(inverses[1])
    hand_on(1, 0)
    hand_on(1, 1)
    handed(1, 0).wait()
    a_out(wa, 0, 4)
    hand_on(1, 2)
    handed(1, 1).wait()
    a_out(wa, 4, A_FULL)
    qa[:, A_FULL * A_STEP :] = normal(wa, joined(1, A_FULL * 4, A_TAIL // LANES))
    handed(1, 2).wait()
    f_out(wf)


def carries(ma, mf, bt, qa, qf, ca, cf, oa, of, sa, sf, sem, q_sem):
    copies = [pltpu.make_async_copy(qa, oa, q_sem.at[0]), pltpu.make_async_copy(qf, of, q_sem.at[1])]
    for copy in copies:
        copy.start()
    bh, bl = split(bt[...])
    basis = jnp.concatenate([bh, bh, bl, bl], axis=0)
    n = 0
    for m, q, out, stage, rows, base, pad, cols, step in (
        (ma, qa, ca, sa, A_ROWS, 0, A_PAD, A_COLS, 512),
        (mf, qf, cf, sf, F_ROWS, A_PAD, F_PAD, F_COLS, 256),
    ):
        for col in range(0, cols, step):
            at = slice(col, min(col + step, cols))
            qh, ql = split(q[:, at])
            low = dot(basis[:, base : base + pad], jnp.concatenate([qh, ql, qh, ql], axis=0), TN)
            full = m[0, :, at].astype(f32) + m[1, :, at].astype(f32) - low
            stage[:, at] = full[:rows]
            copy = pltpu.make_async_copy(stage.at[:, at], out.at[0, :, at], sem.at[n])
            copy.start()
            copies.append(copy)
            n += 1
    for copy in copies:
        copy.wait()


def kernel_one(ag, ae, aw, fg, fe, fw):
    hbm = pl.BlockSpec(memory_space=pl.ANY)
    vmem = pl.BlockSpec(memory_space=pltpu.VMEM)
    dma = pltpu.SemaphoreType.DMA
    return pl.pallas_call(
        sweeps,
        name="sweeps",
        out_shape=(
            pltpu.VMEM((2, A_PAD, A_COLS), bf16),
            pltpu.VMEM((2, F_PAD, F_COLS), bf16),
            pltpu.VMEM((R, ROWS), f32),
            pltpu.VMEM((R, A_COLS), f32),
            pltpu.VMEM((R, F_COLS), f32),
        ),
        in_specs=[hbm] * 6,
        out_specs=[vmem] * 5,
        scratch_shapes=[
            pltpu.VMEM((2, A_ROWS, A_COLS), f32),
            pltpu.VMEM((2, F_ROWS, F_COLS), f32),
            pltpu.VMEM((R, A_COLS), f32),
            pltpu.VMEM((R, F_COLS), f32),
            dma((A_FULL + 1 + F_FULL,)),
            dma((2,)),
            pltpu.VMEM((2 * R, ROWS), f32),
            pltpu.VMEM((2, R, A_PAD), f32),
            pltpu.VMEM((2, R, F_PAD), f32),
            pltpu.VMEM((2, HALF, A_PAD), f32),
            pltpu.VMEM((2, HALF, F_PAD), f32),
            pltpu.VMEM((2, 4, HALF, A_PAD), f32),
            pltpu.VMEM((2, 4, HALF, F_PAD), f32),
            pltpu.VMEM((2, R, A_PAD), f32),
            pltpu.VMEM((2, R, F_PAD), f32),
            pltpu.VMEM((2, PLANE, HALF, LANES), f32),
            pltpu.VMEM((2, 2, UNITS, HALF, LANES), f32),
            pltpu.VMEM((2, UNITS, HALF, LANES), f32),
            pltpu.VMEM((2, UNITS, HALF, LANES), f32),
            pltpu.VMEM((2, CHIPS, HALF, LANES), f32),
            pltpu.VMEM((2, 2, UNITS, HALF, LANES), f32),
            dma((2, 2, 3)),
            dma((2, 2, 3)),
            dma((2,)),
            dma((2,)),
            dma((2, 3)),
            dma((2, 3)),
            dma((2,)),
            dma((2,)),
            dma((2,)),
            dma((2, 3)),
            dma((2, 3)),
            dma((2, 3)),
        ],
        compiler_params=pltpu.CompilerParams(
            collective_id=0, has_side_effects=True, vmem_limit_bytes=46 * 2**20
        ),
    )(ag, ae, fg, fe, aw, fw)


def shards(*args):
    hbm = pl.BlockSpec(memory_space=pl.ANY)
    vmem = pl.BlockSpec(memory_space=pltpu.VMEM)
    dma = pltpu.SemaphoreType.DMA
    return tuple(
        pl.pallas_call(
            carries,
            name="carries",
            out_shape=(
                jax.ShapeDtypeStruct((1, A_ROWS, A_COLS), f32),
                jax.ShapeDtypeStruct((1, F_ROWS, F_COLS), f32),
                jax.ShapeDtypeStruct((R, A_COLS), f32),
                jax.ShapeDtypeStruct((R, F_COLS), f32),
            ),
            in_specs=[vmem] * 5,
            out_specs=[hbm] * 4,
            scratch_shapes=[
                pltpu.VMEM((A_ROWS, A_COLS), f32),
                pltpu.VMEM((F_ROWS, F_COLS), f32),
                dma((16,)),
                dma((2,)),
            ],
            compiler_params=pltpu.CompilerParams(vmem_limit_bytes=24 * 2**20),
        )(*kernel_one(*args))
    )


def solution(mesh):
    rows = P("dp", "shard", None)
    return jax.shard_map(
        shards,
        mesh=mesh,
        in_specs=(rows, rows, P(), rows, rows, P()),
        out_specs=(rows, rows, P(), P()),
        check_vma=False,
    )
```

```python
import functools

import jax
import jax.numpy as jnp
from jax import lax
from jax.experimental import pallas as pl
from jax.experimental.pallas import tpu as pltpu
from jax.sharding import PartitionSpec as P

f32, bf16 = jnp.float32, jnp.bfloat16
MESH = pl.DeviceIdType.MESH
NT = (((1,), (1,)), ((), ()))
NN = (((1,), (0,)), ((), ()))
TN = (((0,), (0,)), ((), ()))

R = 32
HALF = 16
REPLICAS = 8
CHIPS = 64
PLANE = 16
LANES = 128
A_ROWS, A_PAD, A_COLS = 248, 256, 3968
F_ROWS, F_PAD, F_COLS = 496, 512, 2048
ROWS = A_PAD + F_PAD
A_HALF, F_HALF = A_PAD // 2, F_PAD // 2
A_UNITS, F_UNITS = A_COLS // LANES, F_COLS // LANES
F_FIRST, UNITS = 32, 48
A_STEP, F_STEP = 512, 512
A_LOAD, F_LOAD = 1024, 512
A_FULL, A_TAIL = A_COLS // A_STEP, A_COLS % A_STEP
A_LOADS, A_REST = A_COLS // A_LOAD, A_COLS % A_LOAD
F_LOADS = F_COLS // F_LOAD
GROUPS = ((0, 16), (16, 15), (32, 16))


def dot(a, b, dims):
    return lax.dot_general(a, b, dims, preferred_element_type=f32)


def split(x):
    hi = x.astype(bf16)
    return hi, (x - hi.astype(f32)).astype(bf16)


def split3(x):
    hi = x.astype(bf16)
    rest = x - hi.astype(f32)
    mid = rest.astype(bf16)
    return hi, mid, (rest - mid.astype(f32)).astype(bf16)


def applied(inverse, x):
    a, b, c = split3(inverse)
    h, m, l = split3(x)
    return dot(jnp.concatenate([a, a, a, b, b, c], axis=1), jnp.concatenate([h, m, l, h, m, h], axis=0), NN)


def gram_of(x):
    terms = jnp.concatenate(split3(x), axis=0)
    g = dot(terms, terms, NT)
    g = g[:R] + g[R : 2 * R] + g[2 * R :]
    return g[:, :R] + g[:, R : 2 * R] + g[:, 2 * R :]


def stacked(x):
    return jnp.concatenate(split(x), axis=0)


def folded(x):
    return x[:R] + x[R:]


def twice(x):
    terms = stacked(x)
    return jnp.concatenate([terms, terms], axis=1)


def inverse_factors(a):
    lane = lax.broadcasted_iota(jnp.int32, (R, LANES), 1)
    row_of = lax.broadcasted_iota(jnp.int32, (R, LANES), 0)
    for k in range(R):
        row = jnp.broadcast_to(a[k : k + 1, :], (R, LANES))
        first = jnp.broadcast_to(a[:, k : k + 1], (R, LANES))
        second = jnp.broadcast_to(a[:, 64 + k : 65 + k], (R, LANES))
        column = jnp.where(lane < 64, first, second)
        pivot = jnp.broadcast_to(column[k : k + 1, :], (R, LANES))
        factor = jnp.where(row_of > k, column * (1.0 / pivot), 0.0)
        a = a - factor * row
        a = jnp.where(row_of == k, row * lax.rsqrt(pivot), a)
    return a[:, R : 2 * R], a[:, 3 * R :]


def sweeps(
    ag, ae, fg, fe, aw, fw,
    ma, mf, bt, qa, qf,
    sa, sf, swa, swf, load_sem, warm_sem,
    ra, rf, ta, tf, t_send, t_recv,
    acc, a_z, f_z, b_part,
    gs, gt, gm, gz, zl, zp, zs, rr, zg,
    p_send, p_recv, b_send, b_recv, g_send, g_recv, h_send, h_recv, m_send, m_recv,
    rs_send, rs_recv, ag_send, ag_recv, fw_send, fw_recv,
):
    dp, s = lax.axis_index("dp"), lax.axis_index("shard")
    z, c = lax.div(dp, 2), lax.rem(dp, 2)
    x, y = lax.div(s, 4), lax.rem(s, 4)
    j = s * 4 + z
    mate = (z * 2 + (1 - c), s)
    unit = lax.rem(27 * j, CHIPS)
    owner = jnp.logical_and(unit < UNITS, unit != A_UNITS)

    along = [lax.rem(z + i, 4) * 2 + c for i in range(4)]

    def each_peer(act):
        def column(k, _):
            to = lax.rem(x + 2 + lax.div(k, 4), 4) * 4 + lax.rem(y + 2 + lax.rem(k, 4), 4)
            for i in (2, 1, 3):
                act((along[i], to))

            @pl.when(to != s)
            def _():
                act((dp, to))

            return 0

        lax.fori_loop(0, PLANE, column, 0)

    def remote(src, dst, send, recv, to):
        return pltpu.make_async_remote_copy(src, dst, send, recv, device_id=to, device_id_type=MESH)

    def loads(grad, error, stage, col, w, k):
        at = pl.ds(col, w)
        return (
            pltpu.make_async_copy(grad.at[0, :, at], stage.at[0, :, at], load_sem.at[k]),
            pltpu.make_async_copy(error.at[0, :, at], stage.at[1, :, at], load_sem.at[k]),
        )

    load_aw = pltpu.make_async_copy(aw, swa, warm_sem.at[0])
    load_fw = pltpu.make_async_copy(fw, swf, warm_sem.at[1])
    load_aw.start()
    for k in range(A_LOADS + 1):
        for copy in loads(ag, ae, sa, k * A_LOAD, A_LOAD if k < A_LOADS else A_REST, k):
            copy.start()
    load_fw.start()
    for k in range(F_LOADS):
        for copy in loads(fg, fe, sf, k * F_LOAD, F_LOAD, A_LOADS + 1 + k):
            copy.start()

    barrier = pltpu.get_barrier_semaphore()

    def greet(to):
        pl.semaphore_signal(barrier, 1, device_id=to, device_id_type=MESH)

    each_peer(greet)
    pl.semaphore_signal(barrier, 1, device_id=mate, device_id_type=MESH)
    acc[...] = jnp.zeros_like(acc)

    lanes_of = (slice(0, A_PAD), slice(A_PAD, ROWS))

    ma[A_ROWS:] = jnp.zeros((A_PAD - A_ROWS, A_COLS), f32)
    mf[F_ROWS:] = jnp.zeros((F_PAD - F_ROWS, F_COLS), f32)

    def rows_kept(core, m):
        half = (A_HALF, F_HALF)[m]
        return pl.ds(pl.multiple_of(core * half, half), half)

    def half_rows(m, col, w, k):
        at = pl.ds(col, w)
        source = (ma, mf)[m].at[rows_kept(1 - c, m), at]
        return remote(source, (ra, rf)[m].at[:, at], t_send.at[k], t_recv.at[k], mate)

    def absorb(stage, m, rows, col, w, k):
        at = pl.ds(col, w)
        pltpu.make_async_copy(stage.at[:, :, at], stage.at[:, :, at], load_sem.at[k]).wait()
        (ma, mf)[m][:rows, at] = stage[0, :, at] + stage[1, :, at]
        half_rows(m, col, w, k).start()

    def combine(m, col, w, k):
        at = pl.ds(col, w)
        half = (A_HALF, F_HALF)[m]
        half_rows(m, col, w, k).wait()
        both = stacked((ma, mf)[m][rows_kept(c, m), at] + (ra, rf)[m][:, at])
        (ta, tf)[m][:, at] = both
        acc[:, lanes_of[m]] += dot(stacked((swa, swf)[m][:, at]), both, NT)

    def joined(it, first, count):
        return jnp.concatenate(
            [jnp.concatenate([zg[it, 0, first + i], zg[it, 1, first + i]], axis=0) for i in range(count)], axis=1
        )

    def a_left(first, col, w):
        terms = stacked(joined(0, first, w // LANES))
        at = pl.ds(col, w)
        acc[:, lanes_of[0]] += dot(terms, ta[:, at], NT)

    def a_left_step(k, _):
        a_left(k * (A_STEP // LANES), pl.multiple_of(k * A_STEP, A_STEP), A_STEP)
        return 0

    def f_left_step(k, _):
        terms = stacked(joined(0, F_FIRST + k * (F_STEP // LANES), F_STEP // LANES))
        at = pl.ds(pl.multiple_of(k * F_STEP, F_STEP), F_STEP)
        acc[:, lanes_of[1]] += dot(terms, tf[:, at], NT)
        return 0

    along_z = (a_z, f_z)

    def start_z(it, m):
        half = (A_HALF, F_HALF)[m]
        product = folded(acc[:, lanes_of[m]])
        along_z[m][it, z] = product[:, :half] + product[:, half:]
        for i in (2, 1, 3):
            at = along_z[m].at[it, z]
            remote(at, at, p_send.at[it, m], p_recv.at[it, m], (along[i], s)).start()

    def finish_left(it, m, inverses):
        three = along_z[m].at[it, pl.ds(0, 3)]
        remote(three, three, p_send.at[it, m], p_recv.at[it, m], mate).wait()
        terms = along_z[m]
        left = (terms[it, 0] + terms[it, 1]) + (terms[it, 2] + terms[it, 3])
        if it == 1:
            left = applied(inverses[m], left) * (1.0 / REPLICAS)
        return left

    def keep(it, first, product):
        for i in range(product.shape[1] // LANES):
            zl[it, 0, first + i] = product[:HALF, i * LANES : (i + 1) * LANES]
            zl[it, 1, first + i] = product[HALF:, i * LANES : (i + 1) * LANES]

    def right(it, m, terms, first, col, w):
        keep(it, first, folded(dot(terms, (ta, tf)[m][:, pl.ds(col, w)], NN)))

    def right_steps(it, m, terms, begin, end):
        def step(k, _):
            first = k * (A_STEP // LANES) + (0, F_FIRST)[m]
            right(it, m, terms, first, pl.multiple_of(k * A_STEP, A_STEP), A_STEP)
            return 0

        lax.fori_loop(begin, end, step, 0)

    def to_mate(it, g):
        at = pl.ds(*GROUPS[g])
        return remote(zl.at[it, 1 - c, at], zp.at[it, at], m_send.at[it, g], m_recv.at[it, g], mate)

    def scatter(it, g):
        first, count = GROUPS[g]
        to_mate(it, g).wait()
        at = pl.ds(first, count)
        zs[it, at] = zl[it, c, at] + zp[it, at]

        def send(k, _):
            u = first + lax.rem(j + k, count)
            o = lax.rem(19 * u, CHIPS)

            @pl.when(o != j)
            def _():
                to = (lax.rem(o, 4) * 2 + c, lax.div(o, 4))
                remote(zs.at[it, u], rr.at[it, j], rs_send.at[it], rs_recv.at[it], to).start()

            return 0

        lax.fori_loop(0, count, send, 0)

    eye = (lax.broadcasted_iota(jnp.int32, (R, R), 0) == lax.broadcasted_iota(jnp.int32, (R, R), 1)).astype(f32)

    part8, other8 = pl.ds(pl.multiple_of(c * 8, 8), 8), pl.ds(pl.multiple_of((1 - c) * 8, 8), 8)

    def gram_to_mate(it):
        return remote(gt.at[it, other8], gm.at[it], h_send.at[it, 0], h_recv.at[it, 0], mate)

    def start_gram(it, la, lf):
        ga, gf = gram_of(la), gram_of(lf)
        gt[it] = jnp.concatenate([ga[:HALF], ga[HALF:], gf[:HALF], gf[HALF:]], axis=1)
        gram_to_mate(it).start()

    def spread_gram(it):
        gram_to_mate(it).wait()
        gs[it, s] = gt[it, part8] + gm[it]

        def send(k, _):
            at = gs.at[it, s]
            remote(at, at, g_send.at[it], g_recv.at[it], (dp, lax.rem(s + k, PLANE))).start()
            return 0

        lax.fori_loop(1, PLANE, send, 0)

    def finish_gram(it):
        others = gs.at[it, pl.ds(0, PLANE - 1)]
        remote(others, others, g_send.at[it], g_recv.at[it], mate).wait()
        gram = gs[it, 0]
        for o in range(1, PLANE):
            gram = gram + gs[it, o]
        gz[it, part8] = gram
        at = gz.at[it, part8]
        copy = remote(at, at, h_send.at[it, 1], h_recv.at[it, 1], mate)
        copy.start()
        copy.wait_send()
        at = gz.at[it, other8]
        remote(at, at, h_send.at[it, 1], h_recv.at[it, 1], mate).wait_recv()
        gram = gz[it]
        ga = jnp.concatenate([gram[:, :R], gram[:, R : 2 * R]], axis=0)
        gf = jnp.concatenate([gram[:, 2 * R : 3 * R], gram[:, 3 * R :]], axis=0)
        return inverse_factors(jnp.concatenate([ga, eye, gf, eye], axis=1))

    def gather(it):
        @pl.when(owner)
        def _():
            rr[it, j] = zs[it, unit]
            others = rr.at[it, pl.ds(0, CHIPS - 1)]
            remote(others, others, rs_send.at[it], rs_recv.at[it], mate).wait_recv()
            zg[it, c, unit] = jnp.sum(rr[it], axis=0)

            group = lax.div(unit, 16)

            def send(to):
                at = zg.at[it, c, unit]
                remote(at, at, ag_send.at[it], ag_recv.at[it, group], to).start()

            each_peer(send)

    def sent(it):
        @pl.when(owner)
        def _():
            some = zs.at[it, pl.ds(0, 46)]
            remote(some, some, rs_send.at[it], rs_recv.at[it], mate).wait_send()
            others = rr.at[it, pl.ds(0, CHIPS - 1)]
            remote(others, others, ag_send.at[it], rs_recv.at[it], mate).wait_send()

        @pl.when(jnp.logical_not(owner))
        def _():
            some = zs.at[it, pl.ds(0, 47)]
            remote(some, some, rs_send.at[it], rs_recv.at[it], mate).wait_send()

    def handed(it, g):
        first, count = GROUPS[g]
        at = zg.at[it, c, pl.ds(first, count)]
        return remote(at, at, fw_send.at[it, g], fw_recv.at[it, g], mate)

    def hand_on(it, g):
        first, count = GROUPS[g]
        own = jnp.logical_and(unit >= first, unit < first + count)

        @pl.when(own)
        def _():
            some = zg.at[it, c, pl.ds(first, count - 1)]
            remote(some, some, ag_send.at[it], ag_recv.at[it, g], mate).wait_recv()

        @pl.when(jnp.logical_not(own))
        def _():
            some = zg.at[it, c, pl.ds(first, count)]
            remote(some, some, ag_send.at[it], ag_recv.at[it, g], mate).wait_recv()

        handed(it, g).start()

    def normal(inverse, value):
        hi, lo = split(value)
        return dot(inverse, jnp.concatenate([hi, lo, hi, lo], axis=0), NN) * (1.0 / REPLICAS)

    def wide(inverse):
        hi, lo = split(inverse)
        return jnp.concatenate([hi, hi, lo, lo], axis=1)

    def a_out(inverse, begin, end):
        def step(k, _):
            qa[:, pl.ds(pl.multiple_of(k * A_STEP, A_STEP), A_STEP)] = normal(inverse, joined(1, k * 4, 4))
            return 0

        lax.fori_loop(begin, end, step, 0)

    def f_out(inverse):
        def step(k, _):
            qf[:, pl.ds(pl.multiple_of(k * A_STEP, A_STEP), A_STEP)] = normal(inverse, joined(1, F_FIRST + k * 4, 4))
            return 0

        lax.fori_loop(0, F_COLS // A_STEP, step, 0)

    inverses = None
    for it in range(2):
        if it == 0:
            load_aw.wait()
            pl.semaphore_wait(barrier, CHIPS)
            absorb(sa, 0, A_ROWS, 0, A_LOAD, 0)

            def a_first(k, _):
                absorb(sa, 0, A_ROWS, pl.multiple_of(k * A_LOAD, A_LOAD), A_LOAD, k)
                combine(0, pl.multiple_of((k - 1) * A_LOAD, A_LOAD), A_LOAD, k - 1)
                return 0

            lax.fori_loop(1, A_LOADS, a_first, 0)
            absorb(sa, 0, A_ROWS, A_LOADS * A_LOAD, A_REST, A_LOADS)
            combine(0, (A_LOADS - 1) * A_LOAD, A_LOAD, A_LOADS - 1)
            load_fw.wait()
            absorb(sf, 1, F_ROWS, 0, F_LOAD, A_LOADS + 1)
            combine(0, A_LOADS * A_LOAD, A_REST, A_LOADS)
            start_z(it, 0)

            def f_first(k, _):
                absorb(sf, 1, F_ROWS, pl.multiple_of(k * F_LOAD, F_LOAD), F_LOAD, A_LOADS + 1 + k)
                combine(1, pl.multiple_of((k - 1) * F_LOAD, F_LOAD), F_LOAD, A_LOADS + k)
                return 0

            lax.fori_loop(1, F_LOADS, f_first, 0)
            combine(1, (F_LOADS - 1) * F_LOAD, F_LOAD, A_LOADS + F_LOADS)
        else:
            acc[...] = jnp.zeros_like(acc)
            hand_on(0, 0)
            hand_on(0, 1)
            handed(0, 0).wait()
            lax.fori_loop(0, 4, a_left_step, 0)
            hand_on(0, 2)
            handed(0, 1).wait()
            lax.fori_loop(4, A_FULL, a_left_step, 0)
            a_left(A_FULL * (A_STEP // LANES), A_FULL * A_STEP, A_TAIL)
            start_z(it, 0)
            handed(0, 2).wait()
            lax.fori_loop(0, F_COLS // F_STEP, f_left_step, 0)
        start_z(it, 1)
        if it == 1:
            sent(0)
        la = finish_left(it, 0, inverses)
        terms = twice(la)
        right_steps(it, 0, terms, 0, 4)
        to_mate(it, 0).start()
        right_steps(it, 0, terms, 4, A_FULL)
        right(it, 0, terms, A_FULL * (A_STEP // LANES), A_FULL * A_STEP, A_TAIL)
        to_mate(it, 1).start()
        if it == 0:
            scatter(it, 0)
            scatter(it, 1)
        lf = finish_left(it, 1, inverses)
        right_steps(it, 1, twice(lf), 0, F_COLS // A_STEP)
        to_mate(it, 2).start()
        if it == 1:
            scatter(it, 0)
            scatter(it, 1)
        scatter(it, 2)
        start_gram(it, la, lf)
        spread_gram(it)
        gather(it)
        inverses = finish_gram(it)
        if it == 1:
            ba, bf = applied(inverses[0], la), applied(inverses[1], lf)
            b_part[0] = jnp.concatenate([ba, bf], axis=1)
            remote(b_part.at[0], b_part.at[1], b_send.at[0], b_recv.at[0], mate).start()

    def place_basis():
        remote(b_part.at[0], b_part.at[1], b_send.at[0], b_recv.at[0], mate).wait()
        for source, core in ((0, c), (1, 1 - c)):
            bt[:, pl.ds(pl.multiple_of(core * A_HALF, A_HALF), A_HALF)] = b_part[source, :, :A_HALF]
            bt[:, pl.ds(pl.multiple_of(A_PAD + core * F_HALF, A_HALF), F_HALF)] = b_part[source, :, A_HALF:]

    wa, wf = wide(inverses[0]), wide(inverses[1])
    hand_on(1, 0)
    place_basis()
    hand_on(1, 1)
    handed(1, 0).wait()
    a_out(wa, 0, 4)
    hand_on(1, 2)
    handed(1, 1).wait()
    a_out(wa, 4, A_FULL)
    qa[:, A_FULL * A_STEP :] = normal(wa, joined(1, A_FULL * 4, A_TAIL // LANES))
    handed(1, 2).wait()
    f_out(wf)
    sent(1)


def carries(ma, mf, bt, qa, qf, ca, cf, oa, of, sa, sf, sem, q_sem):
    copies = [pltpu.make_async_copy(qa, oa, q_sem.at[0]), pltpu.make_async_copy(qf, of, q_sem.at[1])]
    for copy in copies:
        copy.start()
    bh, bl = split(bt[...])
    basis = jnp.concatenate([bh, bh, bl, bl], axis=0)
    n = 0
    for m, q, out, stage, rows, base, pad, cols, step in (
        (ma, qa, ca, sa, A_ROWS, 0, A_PAD, A_COLS, 512),
        (mf, qf, cf, sf, F_ROWS, A_PAD, F_PAD, F_COLS, 256),
    ):
        for col in range(0, cols, step):
            at = slice(col, min(col + step, cols))
            qh, ql = split(q[:, at])
            low = dot(basis[:, base : base + pad], jnp.concatenate([qh, ql, qh, ql], axis=0), TN)
            stage[:, at] = m[:rows, at] - low[:rows]
            copy = pltpu.make_async_copy(stage.at[:, at], out.at[0, :, at], sem.at[n])
            copy.start()
            copies.append(copy)
            n += 1
    for copy in copies:
        copy.wait()


def kernel_one(ag, ae, aw, fg, fe, fw):
    hbm = pl.BlockSpec(memory_space=pl.ANY)
    vmem = pl.BlockSpec(memory_space=pltpu.VMEM)
    dma = pltpu.SemaphoreType.DMA
    return pl.pallas_call(
        sweeps,
        name="sweeps",
        out_shape=(
            pltpu.VMEM((A_PAD, A_COLS), f32),
            pltpu.VMEM((F_PAD, F_COLS), f32),
            pltpu.VMEM((R, ROWS), f32),
            pltpu.VMEM((R, A_COLS), f32),
            pltpu.VMEM((R, F_COLS), f32),
        ),
        in_specs=[hbm] * 6,
        out_specs=[vmem] * 5,
        scratch_shapes=[
            pltpu.VMEM((2, A_ROWS, A_COLS), f32),
            pltpu.VMEM((2, F_ROWS, F_COLS), f32),
            pltpu.VMEM((R, A_COLS), f32),
            pltpu.VMEM((R, F_COLS), f32),
            dma((A_LOADS + 1 + F_LOADS,)),
            dma((2,)),
            pltpu.VMEM((A_HALF, A_COLS), f32),
            pltpu.VMEM((F_HALF, F_COLS), f32),
            pltpu.VMEM((A_PAD, A_COLS), bf16),
            pltpu.VMEM((F_PAD, F_COLS), bf16),
            dma((A_LOADS + 1 + F_LOADS,)),
            dma((A_LOADS + 1 + F_LOADS,)),
            pltpu.VMEM((2 * R, ROWS), f32),
            pltpu.VMEM((2, 4, R, A_HALF), f32),
            pltpu.VMEM((2, 4, R, F_HALF), f32),
            pltpu.VMEM((2, R, A_HALF + F_HALF), f32),
            pltpu.VMEM((2, PLANE, 8, LANES), f32),
            pltpu.VMEM((2, HALF, LANES), f32),
            pltpu.VMEM((2, 8, LANES), f32),
            pltpu.VMEM((2, HALF, LANES), f32),
            pltpu.VMEM((2, 2, UNITS, HALF, LANES), f32),
            pltpu.VMEM((2, UNITS, HALF, LANES), f32),
            pltpu.VMEM((2, UNITS, HALF, LANES), f32),
            pltpu.VMEM((2, CHIPS, HALF, LANES), f32),
            pltpu.VMEM((2, 2, UNITS, HALF, LANES), f32),
            dma((2, 2)),
            dma((2, 2)),
            dma((1,)),
            dma((1,)),
            dma((2,)),
            dma((2,)),
            dma((2, 2)),
            dma((2, 2)),
            dma((2, 3)),
            dma((2, 3)),
            dma((2,)),
            dma((2,)),
            dma((2,)),
            dma((2, 3)),
            dma((2, 3)),
            dma((2, 3)),
        ],
        compiler_params=pltpu.CompilerParams(
            collective_id=0, has_side_effects=True, vmem_limit_bytes=46 * 2**20
        ),
    )(ag, ae, fg, fe, aw, fw)


def shards(*args):
    hbm = pl.BlockSpec(memory_space=pl.ANY)
    vmem = pl.BlockSpec(memory_space=pltpu.VMEM)
    dma = pltpu.SemaphoreType.DMA
    return tuple(
        pl.pallas_call(
            carries,
            name="carries",
            out_shape=(
                jax.ShapeDtypeStruct((1, A_ROWS, A_COLS), f32),
                jax.ShapeDtypeStruct((1, F_ROWS, F_COLS), f32),
                jax.ShapeDtypeStruct((R, A_COLS), f32),
                jax.ShapeDtypeStruct((R, F_COLS), f32),
            ),
            in_specs=[vmem] * 5,
            out_specs=[hbm] * 4,
            scratch_shapes=[
                pltpu.VMEM((A_ROWS, A_COLS), f32),
                pltpu.VMEM((F_ROWS, F_COLS), f32),
                dma((16,)),
                dma((2,)),
            ],
            compiler_params=pltpu.CompilerParams(vmem_limit_bytes=24 * 2**20),
        )(*kernel_one(*args))
    )


def solution(mesh):
    rows = P("dp", "shard", None)
    return jax.shard_map(
        shards,
        mesh=mesh,
        in_specs=(rows, rows, P(), rows, rows, P()),
        out_specs=(rows, rows, P(), P()),
        check_vma=False,
    )
```

```python
import functools

import jax
import jax.numpy as jnp
from jax import lax
from jax.experimental import pallas as pl
from jax.experimental.pallas import tpu as pltpu
from jax.sharding import PartitionSpec as P

f32, bf16 = jnp.float32, jnp.bfloat16
MESH = pl.DeviceIdType.MESH
NT = (((1,), (1,)), ((), ()))
NN = (((1,), (0,)), ((), ()))
TN = (((0,), (0,)), ((), ()))

R = 32
HALF = 16
REPLICAS = 8
CHIPS = 64
PLANE = 16
LANES = 128
A_ROWS, A_PAD, A_COLS = 248, 256, 3968
F_ROWS, F_PAD, F_COLS = 496, 512, 2048
ROWS = A_PAD + F_PAD
A_HALF, F_HALF = A_PAD // 2, F_PAD // 2
A_UNITS, F_UNITS = A_COLS // LANES, F_COLS // LANES
F_FIRST, UNITS = 32, 48
A_STEP, F_STEP = 512, 512
A_LOAD, F_LOAD = 1024, 512
A_FULL, A_TAIL = A_COLS // A_STEP, A_COLS % A_STEP
A_LOADS, A_REST = A_COLS // A_LOAD, A_COLS % A_LOAD
F_LOADS = F_COLS // F_LOAD
GROUPS = ((0, 16), (16, 15), (32, 16))


def dot(a, b, dims):
    return lax.dot_general(a, b, dims, preferred_element_type=f32)


def split(x):
    hi = x.astype(bf16)
    return hi, (x - hi.astype(f32)).astype(bf16)


def split3(x):
    hi = x.astype(bf16)
    rest = x - hi.astype(f32)
    mid = rest.astype(bf16)
    return hi, mid, (rest - mid.astype(f32)).astype(bf16)


def applied(inverse, x):
    a, b, c = split3(inverse)
    h, m, l = split3(x)
    return dot(jnp.concatenate([a, a, a, b, b, c], axis=1), jnp.concatenate([h, m, l, h, m, h], axis=0), NN)


def gram_of(x):
    terms = jnp.concatenate(split3(x), axis=0)
    g = dot(terms, terms, NT)
    g = g[:R] + g[R : 2 * R] + g[2 * R :]
    return g[:, :R] + g[:, R : 2 * R] + g[:, 2 * R :]


def stacked(x):
    return jnp.concatenate(split(x), axis=0)


def folded(x):
    return x[:R] + x[R:]


def twice(x):
    terms = stacked(x)
    return jnp.concatenate([terms, terms], axis=1)


def inverse_factors(a):
    lane = lax.broadcasted_iota(jnp.int32, (R, LANES), 1)
    row_of = lax.broadcasted_iota(jnp.int32, (R, LANES), 0)
    for k in range(R):
        row = jnp.broadcast_to(a[k : k + 1, :], (R, LANES))
        first = jnp.broadcast_to(a[:, k : k + 1], (R, LANES))
        second = jnp.broadcast_to(a[:, 64 + k : 65 + k], (R, LANES))
        column = jnp.where(lane < 64, first, second)
        pivot = jnp.broadcast_to(column[k : k + 1, :], (R, LANES))
        factor = jnp.where(row_of > k, column * (1.0 / pivot), 0.0)
        a = a - factor * row
        a = jnp.where(row_of == k, row * lax.rsqrt(pivot), a)
    return a[:, R : 2 * R], a[:, 3 * R :]


def sweeps(
    ag, ae, fg, fe, aw, fw,
    ma, mf, bt, qa, qf,
    sa, sf, swa, swf, load_sem, warm_sem,
    ra, rf, ta, tf, t_send, t_recv,
    pa, pf, na, nf, l_send, l_recv,
    acc, a_z, f_z, b_part,
    gs, gt, gm, gz, zl, zp, zs, rr, zg,
    p_send, p_recv, b_send, b_recv, g_send, g_recv, h_send, h_recv, m_send, m_recv,
    rs_send, rs_recv, ag_send, ag_recv, fw_send, fw_recv,
):
    dp, s = lax.axis_index("dp"), lax.axis_index("shard")
    z, c = lax.div(dp, 2), lax.rem(dp, 2)
    x, y = lax.div(s, 4), lax.rem(s, 4)
    j = s * 4 + z
    mate = (z * 2 + (1 - c), s)
    unit = lax.rem(27 * j, CHIPS)
    owner = jnp.logical_and(unit < UNITS, unit != A_UNITS)

    along = [lax.rem(z + i, 4) * 2 + c for i in range(4)]

    def each_peer(act):
        def column(k, _):
            to = lax.rem(x + 2 + lax.div(k, 4), 4) * 4 + lax.rem(y + 2 + lax.rem(k, 4), 4)
            for i in (2, 1, 3):
                act((along[i], to))

            @pl.when(to != s)
            def _():
                act((dp, to))

            return 0

        lax.fori_loop(0, PLANE, column, 0)

    def remote(src, dst, send, recv, to):
        return pltpu.make_async_remote_copy(src, dst, send, recv, device_id=to, device_id_type=MESH)

    def loads(grad, error, stage, col, w, k):
        at = pl.ds(col, w)
        return (
            pltpu.make_async_copy(grad.at[0, :, at], stage.at[0, :, at], load_sem.at[k]),
            pltpu.make_async_copy(error.at[0, :, at], stage.at[1, :, at], load_sem.at[k]),
        )

    load_aw = pltpu.make_async_copy(aw, swa, warm_sem.at[0])
    load_fw = pltpu.make_async_copy(fw, swf, warm_sem.at[1])
    load_aw.start()
    for k in range(A_LOADS + 1):
        for copy in loads(ag, ae, sa, k * A_LOAD, A_LOAD if k < A_LOADS else A_REST, k):
            copy.start()
    load_fw.start()
    for k in range(F_LOADS):
        for copy in loads(fg, fe, sf, k * F_LOAD, F_LOAD, A_LOADS + 1 + k):
            copy.start()

    barrier = pltpu.get_barrier_semaphore()

    def greet(to):
        pl.semaphore_signal(barrier, 1, device_id=to, device_id_type=MESH)

    each_peer(greet)
    pl.semaphore_signal(barrier, 1, device_id=mate, device_id_type=MESH)
    acc[...] = jnp.zeros_like(acc)

    lanes_of = (slice(0, A_PAD), slice(A_PAD, ROWS))

    ma[A_ROWS:] = jnp.zeros((A_PAD - A_ROWS, A_COLS), f32)
    mf[F_ROWS:] = jnp.zeros((F_PAD - F_ROWS, F_COLS), f32)

    def absorb(m, col, w, k):
        stage, rows, pad = ((sa, A_ROWS, A_PAD), (sf, F_ROWS, F_PAD))[m]
        at = pl.ds(col, w)
        pltpu.make_async_copy(stage.at[:, :, at], stage.at[:, :, at], load_sem.at[k]).wait()
        value = stage[0, :, at] + stage[1, :, at]
        (ma, mf)[m][:rows, at] = value
        hi, lo = split(jnp.concatenate([value, jnp.zeros((pad - rows, w), f32)], axis=0))
        terms = stacked((swa, swf)[m][:, at])
        acc[:, lanes_of[m]] += dot(terms, hi, NT) + dot(terms, lo, NT)

    def a_absorb(k, _):
        absorb(0, pl.multiple_of(k * A_LOAD, A_LOAD), A_LOAD, k)
        return 0

    def f_absorb(k, _):
        absorb(1, pl.multiple_of(k * F_LOAD, F_LOAD), F_LOAD, A_LOADS + 1 + k)
        return 0

    def kept(core, m):
        half = (A_HALF, F_HALF)[m]
        return pl.ds(pl.multiple_of(core * half, half), half)

    def half_rows(m):
        return remote((ma, mf)[m].at[kept(1 - c, m)], (ra, rf)[m], t_send.at[m], t_recv.at[m], mate)

    def combine(m):
        half, w, target = ((A_HALF, LANES, ta), (F_HALF, LANES, tf))[m]
        half_rows(m).wait()

        def step(k, _):
            at = pl.ds(pl.multiple_of(k * w, w), w)
            target[:, at] = stacked((ma, mf)[m][kept(c, m), at] + (ra, rf)[m][:, at])
            return 0

        lax.fori_loop(0, (A_COLS, F_COLS)[m] // w, step, 0)

    def half_left(m):
        return remote((pa, pf)[m].at[:, kept(1 - c, m)], (na, nf)[m], l_send.at[m], l_recv.at[m], mate)

    def start_left(m):
        (pa, pf)[m][...] = folded(acc[:, lanes_of[m]])
        half_left(m).start()

    def joined(it, first, count):
        return jnp.concatenate(
            [jnp.concatenate([zg[it, 0, first + i], zg[it, 1, first + i]], axis=0) for i in range(count)], axis=1
        )

    def a_left(first, col, w):
        terms = stacked(joined(0, first, w // LANES))
        at = pl.ds(col, w)
        acc[:, lanes_of[0]] += dot(terms, ta[:, at], NT)

    def a_left_step(k, _):
        a_left(k * (A_STEP // LANES), pl.multiple_of(k * A_STEP, A_STEP), A_STEP)
        return 0

    def f_left_step(k, _):
        terms = stacked(joined(0, F_FIRST + k * (F_STEP // LANES), F_STEP // LANES))
        at = pl.ds(pl.multiple_of(k * F_STEP, F_STEP), F_STEP)
        acc[:, lanes_of[1]] += dot(terms, tf[:, at], NT)
        return 0

    along_z = (a_z, f_z)

    def start_z(it, m):
        half = (A_HALF, F_HALF)[m]
        if it == 0:
            half_left(m).wait()
            along_z[m][it, z] = (pa, pf)[m][:, kept(c, m)] + (na, nf)[m][...]
        else:
            product = folded(acc[:, lanes_of[m]])
            along_z[m][it, z] = product[:, :half] + product[:, half:]
        for i in (2, 1, 3):
            at = along_z[m].at[it, z]
            remote(at, at, p_send.at[it, m], p_recv.at[it, m], (along[i], s)).start()

    def finish_left(it, m, inverses):
        three = along_z[m].at[it, pl.ds(0, 3)]
        remote(three, three, p_send.at[it, m], p_recv.at[it, m], mate).wait()
        terms = along_z[m]
        left = (terms[it, 0] + terms[it, 1]) + (terms[it, 2] + terms[it, 3])
        if it == 1:
            left = applied(inverses[m], left) * (1.0 / REPLICAS)
        return left

    def keep(it, first, product):
        for i in range(product.shape[1] // LANES):
            zl[it, 0, first + i] = product[:HALF, i * LANES : (i + 1) * LANES]
            zl[it, 1, first + i] = product[HALF:, i * LANES : (i + 1) * LANES]

    def right(it, m, terms, first, col, w):
        keep(it, first, folded(dot(terms, (ta, tf)[m][:, pl.ds(col, w)], NN)))

    def right_steps(it, m, terms, begin, end):
        def step(k, _):
            first = k * (A_STEP // LANES) + (0, F_FIRST)[m]
            right(it, m, terms, first, pl.multiple_of(k * A_STEP, A_STEP), A_STEP)
            return 0

        lax.fori_loop(begin, end, step, 0)

    def to_mate(it, g):
        at = pl.ds(*GROUPS[g])
        return remote(zl.at[it, 1 - c, at], zp.at[it, at], m_send.at[it, g], m_recv.at[it, g], mate)

    def scatter(it, g):
        first, count = GROUPS[g]
        to_mate(it, g).wait()
        at = pl.ds(first, count)
        zs[it, at] = zl[it, c, at] + zp[it, at]

        def send(k, _):
            u = first + lax.rem(j + k, count)
            o = lax.rem(19 * u, CHIPS)

            @pl.when(o != j)
            def _():
                to = (lax.rem(o, 4) * 2 + c, lax.div(o, 4))
                remote(zs.at[it, u], rr.at[it, j], rs_send.at[it], rs_recv.at[it], to).start()

            return 0

        lax.fori_loop(0, count, send, 0)

    eye = (lax.broadcasted_iota(jnp.int32, (R, R), 0) == lax.broadcasted_iota(jnp.int32, (R, R), 1)).astype(f32)

    part8, other8 = pl.ds(pl.multiple_of(c * 8, 8), 8), pl.ds(pl.multiple_of((1 - c) * 8, 8), 8)

    def gram_to_mate(it):
        return remote(gt.at[it, other8], gm.at[it], h_send.at[it, 0], h_recv.at[it, 0], mate)

    def start_gram(it, la, lf):
        ga, gf = gram_of(la), gram_of(lf)
        gt[it] = jnp.concatenate([ga[:HALF], ga[HALF:], gf[:HALF], gf[HALF:]], axis=1)
        gram_to_mate(it).start()

    def spread_gram(it):
        gram_to_mate(it).wait()
        gs[it, s] = gt[it, part8] + gm[it]

        def send(k, _):
            at = gs.at[it, s]
            remote(at, at, g_send.at[it], g_recv.at[it], (dp, lax.rem(s + k, PLANE))).start()
            return 0

        lax.fori_loop(1, PLANE, send, 0)

    def finish_gram(it):
        others = gs.at[it, pl.ds(0, PLANE - 1)]
        remote(others, others, g_send.at[it], g_recv.at[it], mate).wait()
        gram = gs[it, 0]
        for o in range(1, PLANE):
            gram = gram + gs[it, o]
        gz[it, part8] = gram
        at = gz.at[it, part8]
        copy = remote(at, at, h_send.at[it, 1], h_recv.at[it, 1], mate)
        copy.start()
        copy.wait_send()
        at = gz.at[it, other8]
        remote(at, at, h_send.at[it, 1], h_recv.at[it, 1], mate).wait_recv()
        gram = gz[it]
        ga = jnp.concatenate([gram[:, :R], gram[:, R : 2 * R]], axis=0)
        gf = jnp.concatenate([gram[:, 2 * R : 3 * R], gram[:, 3 * R :]], axis=0)
        return inverse_factors(jnp.concatenate([ga, eye, gf, eye], axis=1))

    def gather(it):
        @pl.when(owner)
        def _():
            rr[it, j] = zs[it, unit]
            others = rr.at[it, pl.ds(0, CHIPS - 1)]
            remote(others, others, rs_send.at[it], rs_recv.at[it], mate).wait_recv()
            zg[it, c, unit] = jnp.sum(rr[it], axis=0)

            group = lax.div(unit, 16)

            def send(to):
                at = zg.at[it, c, unit]
                remote(at, at, ag_send.at[it], ag_recv.at[it, group], to).start()

            each_peer(send)

    def sent(it):
        @pl.when(owner)
        def _():
            some = zs.at[it, pl.ds(0, 46)]
            remote(some, some, rs_send.at[it], rs_recv.at[it], mate).wait_send()
            others = rr.at[it, pl.ds(0, CHIPS - 1)]
            remote(others, others, ag_send.at[it], rs_recv.at[it], mate).wait_send()

        @pl.when(jnp.logical_not(owner))
        def _():
            some = zs.at[it, pl.ds(0, 47)]
            remote(some, some, rs_send.at[it], rs_recv.at[it], mate).wait_send()

    def handed(it, g):
        first, count = GROUPS[g]
        at = zg.at[it, c, pl.ds(first, count)]
        return remote(at, at, fw_send.at[it, g], fw_recv.at[it, g], mate)

    def hand_on(it, g):
        first, count = GROUPS[g]
        own = jnp.logical_and(unit >= first, unit < first + count)

        @pl.when(own)
        def _():
            some = zg.at[it, c, pl.ds(first, count - 1)]
            remote(some, some, ag_send.at[it], ag_recv.at[it, g], mate).wait_recv()

        @pl.when(jnp.logical_not(own))
        def _():
            some = zg.at[it, c, pl.ds(first, count)]
            remote(some, some, ag_send.at[it], ag_recv.at[it, g], mate).wait_recv()

        handed(it, g).start()

    def normal(inverse, value):
        hi, lo = split(value)
        return dot(inverse, jnp.concatenate([hi, lo, hi, lo], axis=0), NN) * (1.0 / REPLICAS)

    def wide(inverse):
        hi, lo = split(inverse)
        return jnp.concatenate([hi, hi, lo, lo], axis=1)

    def a_out(inverse, begin, end):
        def step(k, _):
            qa[:, pl.ds(pl.multiple_of(k * A_STEP, A_STEP), A_STEP)] = normal(inverse, joined(1, k * 4, 4))
            return 0

        lax.fori_loop(begin, end, step, 0)

    def f_out(inverse):
        def step(k, _):
            qf[:, pl.ds(pl.multiple_of(k * A_STEP, A_STEP), A_STEP)] = normal(inverse, joined(1, F_FIRST + k * 4, 4))
            return 0

        lax.fori_loop(0, F_COLS // A_STEP, step, 0)

    inverses = None
    for it in range(2):
        if it == 0:
            load_aw.wait()
            lax.fori_loop(0, A_LOADS, a_absorb, 0)
            absorb(0, A_LOADS * A_LOAD, A_REST, A_LOADS)
            load_fw.wait()
            lax.fori_loop(0, F_LOADS // 2, f_absorb, 0)
            pl.semaphore_wait(barrier, CHIPS)
            start_left(0)
            half_rows(0).start()
            lax.fori_loop(F_LOADS // 2, F_LOADS, f_absorb, 0)
            start_left(1)
            start_z(it, 0)
        else:
            acc[...] = jnp.zeros_like(acc)
            hand_on(0, 0)
            hand_on(0, 1)
            handed(0, 0).wait()
            lax.fori_loop(0, 4, a_left_step, 0)
            hand_on(0, 2)
            handed(0, 1).wait()
            lax.fori_loop(4, A_FULL, a_left_step, 0)
            a_left(A_FULL * (A_STEP // LANES), A_FULL * A_STEP, A_TAIL)
            start_z(it, 0)
            handed(0, 2).wait()
            lax.fori_loop(0, F_COLS // F_STEP, f_left_step, 0)
        start_z(it, 1)
        if it == 0:
            half_rows(1).start()
            combine(0)
        else:
            sent(0)
        la = finish_left(it, 0, inverses)
        terms = twice(la)
        right_steps(it, 0, terms, 0, 4)
        to_mate(it, 0).start()
        right_steps(it, 0, terms, 4, A_FULL)
        right(it, 0, terms, A_FULL * (A_STEP // LANES), A_FULL * A_STEP, A_TAIL)
        to_mate(it, 1).start()
        if it == 0:
            scatter(it, 0)
            scatter(it, 1)
        if it == 0:
            combine(1)
        lf = finish_left(it, 1, inverses)
        right_steps(it, 1, twice(lf), 0, F_COLS // A_STEP)
        to_mate(it, 2).start()
        if it == 1:
            scatter(it, 0)
            scatter(it, 1)
        scatter(it, 2)
        start_gram(it, la, lf)
        spread_gram(it)
        gather(it)
        inverses = finish_gram(it)
        if it == 1:
            ba, bf = applied(inverses[0], la), applied(inverses[1], lf)
            b_part[0] = jnp.concatenate([ba, bf], axis=1)
            remote(b_part.at[0], b_part.at[1], b_send.at[0], b_recv.at[0], mate).start()

    def place_basis():
        remote(b_part.at[0], b_part.at[1], b_send.at[0], b_recv.at[0], mate).wait()
        for source, core in ((0, c), (1, 1 - c)):
            bt[:, pl.ds(pl.multiple_of(core * A_HALF, A_HALF), A_HALF)] = b_part[source, :, :A_HALF]
            bt[:, pl.ds(pl.multiple_of(A_PAD + core * F_HALF, A_HALF), F_HALF)] = b_part[source, :, A_HALF:]

    wa, wf = wide(inverses[0]), wide(inverses[1])
    hand_on(1, 0)
    place_basis()
    hand_on(1, 1)
    handed(1, 0).wait()
    a_out(wa, 0, 4)
    hand_on(1, 2)
    handed(1, 1).wait()
    a_out(wa, 4, A_FULL)
    qa[:, A_FULL * A_STEP :] = normal(wa, joined(1, A_FULL * 4, A_TAIL // LANES))
    handed(1, 2).wait()
    f_out(wf)
    sent(1)


def carries(ma, mf, bt, qa, qf, ca, cf, oa, of, sa, sf, sem, q_sem):
    copies = [pltpu.make_async_copy(qa, oa, q_sem.at[0]), pltpu.make_async_copy(qf, of, q_sem.at[1])]
    for copy in copies:
        copy.start()
    bh, bl = split(bt[...])
    basis = jnp.concatenate([bh, bh, bl, bl], axis=0)
    n = 0
    for m, q, out, stage, rows, base, pad, cols, step in (
        (ma, qa, ca, sa, A_ROWS, 0, A_PAD, A_COLS, 512),
        (mf, qf, cf, sf, F_ROWS, A_PAD, F_PAD, F_COLS, 256),
    ):
        for col in range(0, cols, step):
            at = slice(col, min(col + step, cols))
            qh, ql = split(q[:, at])
            low = dot(basis[:, base : base + pad], jnp.concatenate([qh, ql, qh, ql], axis=0), TN)
            stage[:, at] = m[:rows, at] - low[:rows]
            copy = pltpu.make_async_copy(stage.at[:, at], out.at[0, :, at], sem.at[n])
            copy.start()
            copies.append(copy)
            n += 1
    for copy in copies:
        copy.wait()


def kernel_one(ag, ae, aw, fg, fe, fw):
    hbm = pl.BlockSpec(memory_space=pl.ANY)
    vmem = pl.BlockSpec(memory_space=pltpu.VMEM)
    dma = pltpu.SemaphoreType.DMA
    return pl.pallas_call(
        sweeps,
        name="sweeps",
        out_shape=(
            pltpu.VMEM((A_PAD, A_COLS), f32),
            pltpu.VMEM((F_PAD, F_COLS), f32),
            pltpu.VMEM((R, ROWS), f32),
            pltpu.VMEM((R, A_COLS), f32),
            pltpu.VMEM((R, F_COLS), f32),
        ),
        in_specs=[hbm] * 6,
        out_specs=[vmem] * 5,
        scratch_shapes=[
            pltpu.VMEM((2, A_ROWS, A_COLS), f32),
            pltpu.VMEM((2, F_ROWS, F_COLS), f32),
            pltpu.VMEM((R, A_COLS), f32),
            pltpu.VMEM((R, F_COLS), f32),
            dma((A_LOADS + 1 + F_LOADS,)),
            dma((2,)),
            pltpu.VMEM((A_HALF, A_COLS), f32),
            pltpu.VMEM((F_HALF, F_COLS), f32),
            pltpu.VMEM((A_PAD, A_COLS), bf16),
            pltpu.VMEM((F_PAD, F_COLS), bf16),
            dma((2,)),
            dma((2,)),
            pltpu.VMEM((R, A_PAD), f32),
            pltpu.VMEM((R, F_PAD), f32),
            pltpu.VMEM((R, A_HALF), f32),
            pltpu.VMEM((R, F_HALF), f32),
            dma((2,)),
            dma((2,)),
            pltpu.VMEM((2 * R, ROWS), f32),
            pltpu.VMEM((2, 4, R, A_HALF), f32),
            pltpu.VMEM((2, 4, R, F_HALF), f32),
            pltpu.VMEM((2, R, A_HALF + F_HALF), f32),
            pltpu.VMEM((2, PLANE, 8, LANES), f32),
            pltpu.VMEM((2, HALF, LANES), f32),
            pltpu.VMEM((2, 8, LANES), f32),
            pltpu.VMEM((2, HALF, LANES), f32),
            pltpu.VMEM((2, 2, UNITS, HALF, LANES), f32),
            pltpu.VMEM((2, UNITS, HALF, LANES), f32),
            pltpu.VMEM((2, UNITS, HALF, LANES), f32),
            pltpu.VMEM((2, CHIPS, HALF, LANES), f32),
            pltpu.VMEM((2, 2, UNITS, HALF, LANES), f32),
            dma((2, 2)),
            dma((2, 2)),
            dma((1,)),
            dma((1,)),
            dma((2,)),
            dma((2,)),
            dma((2, 2)),
            dma((2, 2)),
            dma((2, 3)),
            dma((2, 3)),
            dma((2,)),
            dma((2,)),
            dma((2,)),
            dma((2, 3)),
            dma((2, 3)),
            dma((2, 3)),
        ],
        compiler_params=pltpu.CompilerParams(
            collective_id=0, has_side_effects=True, vmem_limit_bytes=46 * 2**20
        ),
    )(ag, ae, fg, fe, aw, fw)


def shards(*args):
    hbm = pl.BlockSpec(memory_space=pl.ANY)
    vmem = pl.BlockSpec(memory_space=pltpu.VMEM)
    dma = pltpu.SemaphoreType.DMA
    return tuple(
        pl.pallas_call(
            carries,
            name="carries",
            out_shape=(
                jax.ShapeDtypeStruct((1, A_ROWS, A_COLS), f32),
                jax.ShapeDtypeStruct((1, F_ROWS, F_COLS), f32),
                jax.ShapeDtypeStruct((R, A_COLS), f32),
                jax.ShapeDtypeStruct((R, F_COLS), f32),
            ),
            in_specs=[vmem] * 5,
            out_specs=[hbm] * 4,
            scratch_shapes=[
                pltpu.VMEM((A_ROWS, A_COLS), f32),
                pltpu.VMEM((F_ROWS, F_COLS), f32),
                dma((16,)),
                dma((2,)),
            ],
            compiler_params=pltpu.CompilerParams(vmem_limit_bytes=24 * 2**20),
        )(*kernel_one(*args))
    )


def solution(mesh):
    rows = P("dp", "shard", None)
    return jax.shard_map(
        shards,
        mesh=mesh,
        in_specs=(rows, rows, P(), rows, rows, P()),
        out_specs=(rows, rows, P(), P()),
        check_vma=False,
    )
```
